32 devices in a mesh: reach: 8 (over z, y), ens: 4 (over x, core).
Axes of the slice: x: 2, y: 2, z: 4, core: 2. Of those that a mesh axis runs over, the one named last changes fastest.
Arguments:
- adjoint: float32 [16, 3, 64, 1024], P('ens', None, None, 'reach'), may hold values from -6 to 6
- momentum: bfloat16 [16, 2, 64, 1024], P('ens', None, None, 'reach'), may hold values from -6 to 6
- friction: float32 [64, 1024], P(None, 'reach'), may hold values from 10 to 100
- roughness: float32 [128], replicated, may hold values from 0.02 to 0.1
- geometry: float32 [2, 1024], P(None, 'reach'), may hold values from 0.5 to 2
- face_scale: float32 [4, 1024], P(None, 'reach'), may hold values from 0.5 to 2
- vol_blocks: float32 [2, 64, 64], replicated, may hold values from -0.75 to 0.75
- face_blocks: float32 [4, 64, 64], replicated, may hold values from -0.75 to 0.75
- flux_mix: float32 [2, 3, 3], replicated, may hold values from -3.5 to 3.5
- neighbours: int32 [4, 1024], P(None, 'reach'), may hold values from -1 to 1023, as said below
- patch_map: int32 [1024], P('reach'), may hold values from 0 to 127
- patch_owner: int32 [128], replicated, may hold values from 0 to 7, as said below
- wet: int32 [1024], P('reach'), may hold values 0 or 1
Outputs:
- finals: float32 [16, 3, 64, 1024], P('ens', None, None, 'reach')
- owned: float32 [256], P('reach')
The draws below stay inside these ranges and needn't reach their ends.
Inputs may be any that keep to these rules, and one draw needn't show every extreme that they name: `neighbours`: each entry is -1 or an element index at most 32 positions from the element's own index. `patch_owner`: each owner holds at most 32 patches, and some owner holds exactly 32.
All inputs are finite; a program needn't handle non-finite values. No bound on the sum of `wet` on one device may be relied on, other than what follows from the above.
Results may differ from the reference program's by a relative error of at most 0.0003.
Values sent between devices are 32-bit elements; how exact they have to be, the bound alone decides.
A program may use at most 64 MiB of HBM per device.

```python
import math
import jax
import jax.numpy as jnp
from jax import lax

P_SIZE = 64
RIVW = 32
E_DEV = 128
PATCH_DEV = 16
STEPS = 2
OWN_MAX = 32
NE = 1024
MEMBERS = 16
NPATCH = 128
N_REACH = 8


def draw_neighbours(key, part):
    subkeys = jax.random.split(key, 2)
    cells = jnp.arange(NE, dtype=jnp.int32)
    jitter = jax.random.randint(subkeys[0], (2, NE), 0, RIVW // 4 + 1)
    forced = cells % 64 == 5
    jitter = jnp.where(forced[None, :], 0, jitter)
    forward_link = cells + RIVW - jitter[0]
    backward_link = cells - RIVW + jitter[1]
    upper_link = jnp.where(cells % RIVW == RIVW - 1, -1, cells + 1)
    lower_link = jnp.where(cells % RIVW == 0, -1, cells - 1)
    link_table = jnp.stack([forward_link, backward_link, upper_link, lower_link])
    wall_mask = jax.random.randint(subkeys[1], (4, NE), 0, 10) == 0
    wall_mask = wall_mask & jnp.logical_not(forced)[None, :]
    link_table = jnp.where(wall_mask, -1, link_table)
    link_table = jnp.where((link_table < 0) | (link_table >= NE), -1, link_table)
    return link_table.astype(jnp.int32)


def draw_patch_map(key, part):
    patch_len = E_DEV // PATCH_DEV
    cells = jnp.arange(NE, dtype=jnp.int32)
    shift_val = jax.random.randint(key, (NE,), -(patch_len // 4), patch_len // 4 + 1)
    return jnp.clip((cells + shift_val) // patch_len, 0, NPATCH - 1).astype(jnp.int32)


def draw_patch_owner(key, part):
    subkeys = jax.random.split(key, 3)
    owner_count = NE // E_DEV
    slot_count = owner_count * OWN_MAX
    chosen_owner = jax.random.randint(subkeys[0], (), 0, owner_count)
    slot_ids = jnp.arange(slot_count, dtype=jnp.int32)
    ranking = jax.random.permutation(subkeys[1], slot_count).astype(jnp.int32)
    scores = jnp.where(slot_ids // OWN_MAX == chosen_owner, slot_ids - slot_count, ranking)
    ordering = jnp.argsort(scores, stable=True)
    picked = (ordering[:NPATCH] // OWN_MAX).astype(jnp.int32)
    return jax.random.permutation(subkeys[2], picked).astype(jnp.int32)


def place_ends(drawn, stream_key, low, top_value):
    spot = [jax.random.randint(jax.random.fold_in(stream_key, axis), (), 0, length) for axis, length in enumerate(drawn.shape)]
    main_axis = drawn.shape.index(max(drawn.shape))
    beside = spot[:main_axis] + [(spot[main_axis] + 1) % drawn.shape[main_axis]] + spot[main_axis + 1:]
    return drawn.at[tuple(spot)].set(low).at[tuple(beside)].set(top_value)


def levels(key, shape, cuts, low, high):
    factor_of = 1.0
    for dim, shards_of in cuts:
        steps = jax.random.uniform(jax.random.fold_in(jax.random.fold_in(key, 6), dim), (shards_of,), jnp.float32, low / len(cuts), high / len(cuts))
        factor_of = factor_of * jnp.repeat(jnp.exp(steps), shape[dim] // shards_of).reshape((-1,) + (1,) * (len(shape) - 1 - dim))
    return factor_of


def gaussian(key, dims, spread, bound, pieces=(), kind=jnp.bfloat16):
    result = jax.random.normal(key, dims, jnp.float32) * spread
    if len(pieces) > 0:
        result = levels(key, dims, pieces, -0.22, 0.18) * result
    return jnp.clip(result, min=-bound, max=bound).astype(kind)


def setup_inputs(seed: int = 0) -> dict:
    splits = jax.random.split(jax.random.key(seed), 14)
    return {
        "adjoint": gaussian(splits[0], (MEMBERS, 3, P_SIZE, NE), 1.0, 6.0, ((0, 4), (3, 8)), jnp.float32),
        "momentum": gaussian(splits[1], (MEMBERS, 2, P_SIZE, NE), 1.0, 6.0, ((0, 4), (3, 8))),
        "friction": jnp.clip(jnp.exp(math.log(100.0) - 2.3025851 * jax.random.uniform(splits[2], (P_SIZE, NE), jnp.float32) ** levels(splits[2], (P_SIZE, NE), ((1, 8),), -0.2, 0.2)), 10.0, 100.0),
        "roughness": jnp.clip(jnp.exp(jax.random.uniform(splits[3], (NPATCH,), jnp.float32, math.log(0.02), math.log(0.1))), 0.02, 0.1),
        "geometry": jnp.clip(0.5 + 1.5 * jax.random.uniform(splits[4], (2, NE), jnp.float32) ** levels(splits[4], (2, NE), ((1, 8),), -0.2, 0.2), 0.5, 2.0),
        "face_scale": jnp.clip(jnp.exp(math.log(2.0) - 1.3862944 * jax.random.uniform(splits[5], (4, NE), jnp.float32) ** levels(splits[5], (4, NE), ((1, 8),), -0.2, 0.2)), 0.5, 2.0),
        "vol_blocks": gaussian(splits[6], (2, P_SIZE, P_SIZE), P_SIZE ** -0.5, 0.75, (), jnp.float32),
        "face_blocks": gaussian(splits[7], (4, P_SIZE, P_SIZE), P_SIZE ** -0.5, 0.75, (), jnp.float32),
        "flux_mix": gaussian(splits[8], (2, 3, 3), 3 ** -0.5, 3.5, (), jnp.float32),
        "neighbours": draw_neighbours(jax.random.fold_in(splits[13], 71), 0),
        "patch_map": draw_patch_map(jax.random.fold_in(splits[13], 71), 0),
        "patch_owner": draw_patch_owner(jax.random.fold_in(splits[13], 71), 0),
        "wet": place_ends((jax.random.randint(splits[12], (NE,), 0, 4) < 3).astype(jnp.int32), jax.random.fold_in(splits[12], 1), 0, 1),
    }


TIME_STEP = 0.05
FINEST = lax.Precision.HIGHEST


def apply_block(block, values):
    return jnp.einsum('qp,mcpe->mcqe', block, values, precision=FINEST)


def mix_flux(matrix, values):
    return jnp.einsum('dc,mdpe->mcpe', matrix, values, precision=FINEST)


def adjoint_rhs(lam_ext, anchor, offset, extent, links, geo_sel, face_sel, coef_sel, wet_sel, vol_blocks, face_blocks, flux_mix):
    inside = lax.slice_in_dim(lam_ext, offset, offset + extent, axis=3)
    summed = geo_sel[0] * apply_block(vol_blocks[0], mix_flux(flux_mix[0], inside))
    summed = summed + geo_sel[1] * apply_block(vol_blocks[1], mix_flux(flux_mix[1], inside))
    span_len = lam_ext.shape[3]
    for face_id in range(4):
        target = links[face_id]
        position = jnp.clip(target - anchor, 0, span_len - 1).astype(jnp.int32)
        remote = jnp.take(lam_ext, position, axis=3)
        jump_val = jnp.where(target >= 0, remote - inside, jnp.zeros_like(inside))
        summed = summed + face_sel[face_id] * apply_block(face_blocks[face_id], jump_val)
    damping = -coef_sel * inside[:, 1:3]
    summed = summed + jnp.concatenate([jnp.zeros_like(inside[:, :1]), damping], axis=1)
    return wet_sel * summed


def friction_work(adjoint_now, moment, weights):
    return jnp.sum(weights * (moment[:, 0] * adjoint_now[:, 1] + moment[:, 1] * adjoint_now[:, 2]), axis=1)


def owner_slots(patch_owner, owner_count, capacity):
    table = (patch_owner[:, None] == jnp.arange(owner_count, dtype=jnp.int32)[None, :]).astype(jnp.int32)
    ranks = jnp.cumsum(table, axis=0) - 1
    ranking = jnp.sum(ranks * table, axis=1)
    return (patch_owner * capacity + ranking).astype(jnp.int32)


def reference(adjoint, momentum, friction, roughness, geometry, face_scale, vol_blocks, face_blocks, flux_mix, neighbours, patch_map, patch_owner, wet):
    patch_rough = roughness[patch_map]
    coef_all = patch_rough[None, :] ** 2 * friction
    wet_all = wet.astype(jnp.float32)
    weights = wet_all * (-2.0 * patch_rough) * friction

    def member(member_pair):
        adjoint_now = member_pair[0][None]
        moment = member_pair[1][None].astype(jnp.float32)
        accrued = jnp.zeros((1, NE), jnp.float32)
        for step_no in range(STEPS):
            accrued = accrued + friction_work(adjoint_now, moment, weights)
            slope = adjoint_rhs(adjoint_now, 0, 0, NE, neighbours, geometry, face_scale, coef_all, wet_all, vol_blocks, face_blocks, flux_mix)
            halfway = adjoint_now + TIME_STEP * slope
            accrued = accrued + friction_work(halfway, moment, weights)
            slope = adjoint_rhs(halfway, 0, 0, NE, neighbours, geometry, face_scale, coef_all, wet_all, vol_blocks, face_blocks, flux_mix)
            adjoint_now = 0.5 * adjoint_now + 0.5 * (halfway + TIME_STEP * slope)
        return adjoint_now[0], accrued[0]

    finals, accrued = lax.map(member, (adjoint, momentum))
    per_element = jnp.sum(accrued, axis=0)
    patch_sums = jax.ops.segment_sum(per_element, patch_map, num_segments=NPATCH) / (MEMBERS * P_SIZE)
    slots = owner_slots(patch_owner, N_REACH, OWN_MAX)
    owned = jnp.zeros((N_REACH * OWN_MAX,), jnp.float32).at[slots].set(patch_sums)
    return (finals, owned)
```

```python
import functools

import jax
import jax.numpy as jnp
from jax import lax
from jax.experimental import pallas as pl
from jax.experimental.pallas import tpu as pltpu
from jax.sharding import PartitionSpec as P

RIVW = 32
STEPS = 2
OWN_MAX = 32
TIME_STEP = 0.05
F32 = jnp.float32
BF16 = jnp.bfloat16
FINEST = lax.Precision.HIGHEST
NAMED = pl.DeviceIdType.MESH


def split_two(x):
    hi = x.astype(BF16)
    return hi, (x - hi.astype(F32)).astype(BF16)


def radices(count):
    out = []
    while count > 1:
        size = next(r for r in (8, 7, 6, 5, 4, 3, 2, count) if count % r == 0)
        out.append(size)
        count //= size
    return out


def kernel(
    n_reach, n_ens, members_all,
    adj_ref, mom_ref, fric_ref, rough_ref, geo_ref, face_ref, vol_ref, fb_ref, mix_ref,
    nb_ref, pm_ref, po_ref, wet_ref,
    out_ref, own_ref,
    lam, hal, acc, sel, w_all, dscale, damp, onehot, snd, rcv, psnd, prcv,
    snd_sem, rcv_sem, psnd_sem, prcv_sem,
):
    members, comps, nodes, elems = adj_ref.shape
    npatch = rough_ref.shape[1]
    me = lax.axis_index("reach")
    my_ens = lax.axis_index("ens")
    groups = elems // RIVW
    prows = nodes // groups
    digits = radices(n_reach)

    phases = [("ens", n_ens, my_ens, 1)]
    stride = 1
    for size in digits:
        phases.append(("reach", size, lax.rem(lax.div(me, stride), size), stride))
        stride *= size

    def partner(phase, k):
        axis, size, mine, step = phases[phase]
        other = lax.rem(mine + k, size)
        base = my_ens if axis == "ens" else me
        return {axis: base + (other - mine) * step}

    barrier = pltpu.get_barrier_semaphore()
    expected = 0
    for phase in range(len(phases)):
        for k in range(1, phases[phase][1]):
            pl.semaphore_signal(barrier, inc=1, device_id=partner(phase, k), device_id_type=NAMED)
            expected += 1
    far = len(digits) > 1
    if far:
        @pl.when(me > 0)
        def _():
            pl.semaphore_signal(barrier, inc=1, device_id={"reach": me - 1}, device_id_type=NAMED)

        @pl.when(me < n_reach - 1)
        def _():
            pl.semaphore_signal(barrier, inc=1, device_id={"reach": me + 1}, device_id_type=NAMED)

    lane = lax.broadcasted_iota(jnp.int32, (prows, elems), 1)

    def halo_copy(stage, side, m):
        to = me + 1 if side == 0 else me - 1
        return pltpu.make_async_remote_copy(
            src_ref=snd.at[stage, side, m],
            dst_ref=rcv.at[stage, side, m],
            send_sem=snd_sem.at[stage, side, m],
            recv_sem=rcv_sem.at[stage, side, m],
            device_id={"reach": to},
            device_id_type=NAMED,
        )

    def pack(stage, m, c, x):
        for side in range(2):
            packed = None
            for g in range(groups):
                rows = x[g * prows:(g + 1) * prows]
                shift = (RIVW * g - (elems - RIVW if side == 0 else 0)) % elems
                moved = pltpu.roll(rows, shift, 1) if shift else rows
                packed = moved if packed is None else jnp.where(lane >= g * RIVW, moved, packed)
            snd[stage, side, m, c * prows:(c + 1) * prows, :] = packed

    def send(stage, m):
        @pl.when(me < n_reach - 1)
        def _():
            halo_copy(stage, 0, m).start()

        @pl.when(me > 0)
        def _():
            halo_copy(stage, 1, m).start()

    def receive(stage, m):
        @pl.when(me > 0)
        def _():
            halo_copy(stage, 0, m).wait_recv()

        @pl.when(me < n_reach - 1)
        def _():
            halo_copy(stage, 1, m).wait_recv()

    def work(m, c, x):
        if c == 0:
            return None
        return mom_ref[m, c - 1].astype(F32) * x

    for m in range(members):
        for c in range(comps):
            pack(0, m, c, adj_ref[m, c])

    pl.semaphore_wait(barrier, expected)
    if far:
        @pl.when(me > 0)
        def _():
            pl.semaphore_wait(barrier, 1)

        @pl.when(me < n_reach - 1)
        def _():
            pl.semaphore_wait(barrier, 1)
    for m in range(members):
        send(0, m)

    @pl.when(me == 0)
    def _():
        rcv[:, 0] = jnp.zeros(rcv.shape[:1] + rcv.shape[2:], F32)

    @pl.when(me == n_reach - 1)
    def _():
        rcv[:, 1] = jnp.zeros(rcv.shape[:1] + rcv.shape[2:], F32)

    wet = wet_ref[...].astype(F32)
    wet_dt = TIME_STEP * wet
    patch_row = lax.broadcasted_iota(jnp.int32, (npatch, elems), 0)
    onehot[...] = jnp.where(patch_row == pm_ref[...], 1.0, 0.0).astype(F32)
    rough8 = jnp.broadcast_to(rough_ref[...], (8, npatch))
    rough = jnp.dot(rough8, onehot[...], precision=FINEST, preferred_element_type=F32)[0:1]
    damp[...] = (wet_dt * rough * rough) * fric_ref[...]
    for d in range(2):
        dscale[d:d + 1, :] = wet_dt * geo_ref[d:d + 1, :]
    for f in range(4):
        dscale[2 + f:3 + f, :] = wet_dt * face_ref[f:f + 1, :]

    src_row = lax.broadcasted_iota(jnp.int32, (2 * elems, elems), 0)
    src_col = lax.broadcasted_iota(jnp.int32, (2 * elems, elems), 1)
    itself = jnp.where(src_row == src_col, 1.0, 0.0)
    for f in range(4):
        nb = nb_ref[f:f + 1, :]
        local = nb - me * elems
        row = jnp.where(local < 0, local + elems + RIVW, jnp.where(local < elems, local, local + elems - RIVW))
        row = jnp.where(nb >= 0, row, -1)
        hit = jnp.where(src_row == row, 1.0, 0.0)
        own = jnp.where(nb >= 0, 1.0, 0.0) * itself
        sel[:, f * elems:(f + 1) * elems] = (hit - own).astype(BF16)

    for b in range(6):
        block = vol_ref[b] if b < 2 else fb_ref[b - 2]
        hi, lo = split_two(block)
        w_all[0:nodes, b * nodes:(b + 1) * nodes] = hi
        w_all[nodes:2 * nodes, b * nodes:(b + 1) * nodes] = lo

    first = None
    for m in range(members):
        for c in range(1, comps):
            term = work(m, c, adj_ref[m, c])
            first = term if first is None else first + term
    acc[...] = first

    mix = [[[mix_ref[d, a, c] for c in range(comps)] for a in range(comps)] for d in range(2)]

    def body(stage, src, m):
        receive(stage, m)
        state = [src[m, c] for c in range(comps)]
        ghost = []
        for c in range(comps):
            west = rcv[stage, 0, m, c * prows:(c + 1) * prows, :]
            east = rcv[stage, 1, m, c * prows:(c + 1) * prows, :]
            for g in range(groups):
                a, b = (-RIVW * g) % elems, (elems - RIVW - RIVW * g) % elems
                wr = pltpu.roll(west, a, 1) if a else west
                er = pltpu.roll(east, b, 1) if b else east
                ghost.append(jnp.where(lane < elems // 2, wr, er))
        full = jnp.concatenate(
            [jnp.concatenate(state, axis=0), jnp.concatenate(ghost, axis=0)], axis=1
        )
        hi, lo = split_two(full)
        jump = jnp.dot(hi, sel[...], preferred_element_type=F32)
        jump = jump + jnp.dot(lo, sel[...], preferred_element_type=F32)
        cols_hi, cols_lo = [], []
        for c in range(comps):
            pieces = []
            for d in range(2):
                z = mix[d][0][c] * state[0] + mix[d][1][c] * state[1] + mix[d][2][c] * state[2]
                pieces.append(dscale[d:d + 1, :] * z)
            for f in range(4):
                pieces.append(
                    dscale[2 + f:3 + f, :]
                    * jump[c * nodes:(c + 1) * nodes, f * elems:(f + 1) * elems]
                )
            data = jnp.concatenate(pieces, axis=0)
            dh, dl = split_two(data)
            cols_hi.append(dh)
            cols_lo.append(dl)
        data_hi = jnp.concatenate(cols_hi, axis=1)
        data_lo = jnp.concatenate(cols_lo, axis=1)
        both = jnp.dot(w_all[...], data_hi, preferred_element_type=F32)
        total = both[:nodes] + both[nodes:]
        total = total + jnp.dot(w_all[0:nodes, :], data_lo, preferred_element_type=F32)
        moved = []
        for c in range(comps):
            inc = total[:, c * elems:(c + 1) * elems]
            if c > 0:
                inc = inc - damp[...] * state[c]
            moved.append(state[c] + inc)
        return moved

    last = 2 * STEPS - 1

    def stage_member(stage, m):
        step, half = divmod(stage, 2)
        base = adj_ref if step == 0 else lam
        if half == 0:
            new = body(stage, base, m)
            for c in range(comps):
                hal[m, c] = new[c]
        else:
            new = body(stage, hal, m)
            new = [0.5 * base[m, c] + 0.5 * new[c] for c in range(comps)]
            dst = out_ref if stage == last else lam
            for c in range(comps):
                dst[m, c] = new[c]
        if stage < last:
            for c in range(comps):
                pack(stage + 1, m, c, new[c])
            send(stage + 1, m)
            acc[...] += work(m, 1, new[1]) + work(m, 2, new[2])

    def run(stage, lo, hi):
        def step(m, carry):
            stage_member(stage, m)
            return carry

        lax.fori_loop(lo, hi, step, 0)

    def patch_copy(phase, k):
        mine = phases[phase][2]
        return pltpu.make_async_remote_copy(
            src_ref=psnd.at[phase],
            dst_ref=prcv.at[phase, mine],
            send_sem=psnd_sem.at[phase, k],
            recv_sem=prcv_sem.at[phase, k],
            device_id=partner(phase, k),
            device_id_type=NAMED,
        )

    def patch_send(phase, value):
        psnd[phase] = value
        prcv[phase, phases[phase][2]] = value
        for k in range(1, phases[phase][1]):
            patch_copy(phase, k).start()

    def patch_sum(phase):
        for k in range(1, phases[phase][1]):
            patch_copy(phase, k).wait_recv()
        total = prcv[phase, 0]
        for k in range(1, phases[phase][1]):
            total = total + prcv[phase, k]
        return total

    for stage in range(last):
        run(stage, 0, members)

    per_element = jnp.sum(fric_ref[...] * acc[...], axis=0, keepdims=True) * (-2.0 * wet * rough)
    sums = lax.dot_general(
        jnp.broadcast_to(per_element, (8, elems)), onehot[...], (((1,), (1,)), ((), ())),
        precision=FINEST, preferred_element_type=F32,
    )
    patch_send(0, sums)
    half_way = members // 2
    run(last, 0, half_way)
    for phase in range(1, len(phases)):
        patch_send(phase, patch_sum(phase - 1))
    run(last, half_way, members)
    sums = patch_sum(len(phases) - 1) * (1.0 / (members_all * nodes))

    slot_lanes = 128
    chunk = min(npatch, 128)
    tri = jnp.where(
        lax.broadcasted_iota(jnp.int32, (chunk, chunk), 0)
        < lax.broadcasted_iota(jnp.int32, (chunk, chunk), 1), 1.0, 0.0,
    )
    slot = lax.broadcasted_iota(jnp.int32, (slot_lanes, chunk), 0).astype(F32)
    before = jnp.zeros((1, 1), F32)
    result = jnp.zeros((8, slot_lanes), F32)
    for k in range(npatch // chunk):
        mine = jnp.where(po_ref[:, k * chunk:(k + 1) * chunk] == me, 1.0, 0.0)
        rank = jnp.dot(jnp.broadcast_to(mine, (8, chunk)), tri, preferred_element_type=F32)[0:1] + before
        table = jnp.where(slot == rank, 1.0, 0.0) * mine
        result = result + lax.dot_general(
            sums[:, k * chunk:(k + 1) * chunk], table, (((1,), (1,)), ((), ())),
            precision=FINEST, preferred_element_type=F32,
        )
        before = before + jnp.sum(mine, axis=1, keepdims=True)
    own_ref[...] = result[0:1, :OWN_MAX]

    for stage in range(2 * STEPS):
        for m in range(members):
            @pl.when(me < n_reach - 1)
            def _(stage=stage, m=m):
                halo_copy(stage, 0, m).wait_send()

            @pl.when(me > 0)
            def _(stage=stage, m=m):
                halo_copy(stage, 1, m).wait_send()
    for phase in range(len(phases)):
        for k in range(1, phases[phase][1]):
            patch_copy(phase, k).wait_send()


def shards(
    n_reach, n_ens,
    adjoint, momentum, friction, roughness, geometry, face_scale, vol_blocks, face_blocks,
    flux_mix, neighbours, patch_map, patch_owner, wet,
):
    members, comps, nodes, elems = adjoint.shape
    npatch = roughness.shape[0]
    stages = 2 * STEPS
    prow = comps * nodes * RIVW // elems
    sizes = [n_ens] + radices(n_reach)
    vmem = pl.BlockSpec(memory_space=pltpu.VMEM)
    specs = [vmem] * 13
    specs[8] = pl.BlockSpec(memory_space=pltpu.SMEM)
    finals, owned = pl.pallas_call(
        functools.partial(kernel, n_reach, n_ens, members * n_ens),
        out_shape=(
            jax.ShapeDtypeStruct(adjoint.shape, F32),
            jax.ShapeDtypeStruct((1, OWN_MAX), F32),
        ),
        in_specs=specs,
        out_specs=(vmem, vmem),
        scratch_shapes=[
            pltpu.VMEM(adjoint.shape, F32),
            pltpu.VMEM(adjoint.shape, F32),
            pltpu.VMEM((nodes, elems), F32),
            pltpu.VMEM((2 * elems, 4 * elems), BF16),
            pltpu.VMEM((2 * nodes, 6 * nodes), BF16),
            pltpu.VMEM((8, elems), F32),
            pltpu.VMEM((nodes, elems), F32),
            pltpu.VMEM((npatch, elems), F32),
            pltpu.VMEM((stages, 2, members, prow, elems), F32),
            pltpu.VMEM((stages, 2, members, prow, elems), F32),
            pltpu.VMEM((len(sizes), 8, npatch), F32),
            pltpu.VMEM((len(sizes), max(sizes), 8, npatch), F32),
            pltpu.SemaphoreType.DMA((stages, 2, members)),
            pltpu.SemaphoreType.DMA((stages, 2, members)),
            pltpu.SemaphoreType.DMA((len(sizes), max(sizes))),
            pltpu.SemaphoreType.DMA((len(sizes), max(sizes))),
        ],
        compiler_params=pltpu.CompilerParams(
            collective_id=0, has_side_effects=True, vmem_limit_bytes=40 * 1024 * 1024
        ),
    )(
        adjoint, momentum, friction, roughness.reshape(1, npatch), geometry, face_scale,
        vol_blocks, face_blocks, flux_mix, neighbours, patch_map.reshape(1, elems),
        patch_owner.reshape(1, npatch), wet.reshape(1, elems),
    )
    return finals, owned.reshape(OWN_MAX)


def solution(mesh):
    return jax.shard_map(
        functools.partial(shards, mesh.shape["reach"], mesh.shape["ens"]),
        mesh=mesh,
        in_specs=(
            P("ens", None, None, "reach"),
            P("ens", None, None, "reach"),
            P(None, "reach"),
            P(),
            P(None, "reach"),
            P(None, "reach"),
            P(),
            P(),
            P(),
            P(None, "reach"),
            P("reach"),
            P(),
            P("reach"),
        ),
        out_specs=(P("ens", None, None, "reach"), P("reach")),
        check_vma=False,
    )
```

```python
import functools

import jax
import jax.numpy as jnp
from jax import lax
from jax.experimental import pallas as pl
from jax.experimental.pallas import tpu as pltpu
from jax.sharding import PartitionSpec as P

RIVW = 32
STEPS = 2
OWN_MAX = 32
TIME_STEP = 0.05
F32 = jnp.float32
BF16 = jnp.bfloat16
GROUP = 1
FINEST = lax.Precision.HIGHEST
NAMED = pl.DeviceIdType.MESH


def split_two(x):
    hi = x.astype(BF16)
    return hi, (x - hi.astype(F32)).astype(BF16)


def radices(count):
    out = []
    while count > 1:
        size = next(r for r in (8, 7, 6, 5, 4, 3, 2, count) if count % r == 0)
        out.append(size)
        count //= size
    return out


def kernel(
    n_reach, n_ens, members_all,
    adj_hbm, mom_hbm, fric_hbm, rough_hbm, geo_hbm, face_hbm, vol_hbm, fb_hbm, mix_hbm,
    nb_hbm, pm_hbm, po_hbm, wet_hbm,
    out_ref, own_ref,
    mom_ref, fric_ref, rough_ref, geo_ref, face_ref, vol_ref, fb_ref, mix_ref,
    nb_ref, pm_ref, po_ref, wet_ref, in_sem,
    lam, hal, acc, sel, w_all, dscale, damp, onehot, snd, rcv, psnd, prcv,
    snd_sem, rcv_sem, psnd_sem, prcv_sem, table, out_sem,
):
    members, comps, nodes, elems = lam.shape
    npatch = rough_ref.shape[1]
    me = lax.axis_index("reach")
    my_ens = lax.axis_index("ens")
    groups = elems // RIVW
    prows = nodes // groups
    digits = radices(n_reach)

    phases = [("ens", n_ens, my_ens, 1)]
    stride = 1
    for size in digits:
        phases.append(("reach", size, lax.rem(lax.div(me, stride), size), stride))
        stride *= size

    def partner(phase, k):
        axis, size, mine, step = phases[phase]
        other = lax.rem(mine + k, size)
        base = my_ens if axis == "ens" else me
        return {axis: base + (other - mine) * step}

    barrier = pltpu.get_barrier_semaphore()
    expected = 0
    for phase in range(len(phases)):
        for k in range(1, phases[phase][1]):
            pl.semaphore_signal(barrier, inc=1, device_id=partner(phase, k), device_id_type=NAMED)
            expected += 1
    far = len(digits) > 1
    if far:
        @pl.when(me > 0)
        def _():
            pl.semaphore_signal(barrier, inc=1, device_id={"reach": me - 1}, device_id_type=NAMED)

        @pl.when(me < n_reach - 1)
        def _():
            pl.semaphore_signal(barrier, inc=1, device_id={"reach": me + 1}, device_id_type=NAMED)

    state_in = [
        pltpu.make_async_copy(adj_hbm.at[m], lam.at[m], in_sem.at[m]) for m in range(members)
    ]
    tables_in = [
        pltpu.make_async_copy(src, dst, in_sem.at[members + i])
        for i, (src, dst) in enumerate([
            (nb_hbm, nb_ref), (pm_hbm, pm_ref), (rough_hbm, rough_ref), (wet_hbm, wet_ref),
            (fric_hbm, fric_ref), (geo_hbm, geo_ref), (face_hbm, face_ref),
            (vol_hbm, vol_ref), (fb_hbm, fb_ref), (mom_hbm, mom_ref), (mix_hbm, mix_ref),
            (po_hbm, po_ref),
        ])
    ]
    for copy in state_in + tables_in:
        copy.start()

    lane = lax.broadcasted_iota(jnp.int32, (prows, elems), 1)

    def halo_copy(stage, side, m):
        to = me + 1 if side == 0 else me - 1
        return pltpu.make_async_remote_copy(
            src_ref=snd.at[stage, side, m],
            dst_ref=rcv.at[stage, side, m],
            send_sem=snd_sem.at[stage, side, m],
            recv_sem=rcv_sem.at[stage, side, m],
            device_id={"reach": to},
            device_id_type=NAMED,
        )

    def pack(stage, m, c, x):
        for side in range(2):
            packed = None
            for g in range(groups):
                rows = x[g * prows:(g + 1) * prows]
                shift = (RIVW * g - (elems - RIVW if side == 0 else 0)) % elems
                moved = pltpu.roll(rows, shift, 1) if shift else rows
                packed = moved if packed is None else jnp.where(lane >= g * RIVW, moved, packed)
            snd[stage, side, m, c * prows:(c + 1) * prows, :] = packed

    def send(stage, m):
        @pl.when(me < n_reach - 1)
        def _():
            halo_copy(stage, 0, m).start()

        @pl.when(me > 0)
        def _():
            halo_copy(stage, 1, m).start()

    def receive(stage, m):
        @pl.when(me > 0)
        def _():
            halo_copy(stage, 0, m).wait_recv()

        @pl.when(me < n_reach - 1)
        def _():
            halo_copy(stage, 1, m).wait_recv()

    def work(m, c, x):
        if c == 0:
            return None
        return mom_ref[m, c - 1].astype(F32) * x

    for m in range(members):
        state_in[m].wait()
        for c in range(comps):
            pack(0, m, c, lam[m, c])
        if m == 0:
            pl.semaphore_wait(barrier, expected)
            if far:
                @pl.when(me > 0)
                def _():
                    pl.semaphore_wait(barrier, 1)

                @pl.when(me < n_reach - 1)
                def _():
                    pl.semaphore_wait(barrier, 1)
        send(0, m)

    @pl.when(me == 0)
    def _():
        rcv[:, 0] = jnp.zeros(rcv.shape[:1] + rcv.shape[2:], F32)

    @pl.when(me == n_reach - 1)
    def _():
        rcv[:, 1] = jnp.zeros(rcv.shape[:1] + rcv.shape[2:], F32)

    for copy in tables_in:
        copy.wait()
    wet = wet_ref[...].astype(F32)
    wet_dt = TIME_STEP * wet
    patch_row = lax.broadcasted_iota(jnp.int32, (npatch, elems), 0)
    onehot[...] = jnp.where(patch_row == pm_ref[...], 1.0, 0.0).astype(F32)
    rough8 = jnp.broadcast_to(rough_ref[...], (8, npatch))
    rough = jnp.dot(rough8, onehot[...], precision=FINEST, preferred_element_type=F32)[0:1]
    damp[...] = (wet_dt * rough * rough) * fric_ref[...]
    for d in range(2):
        dscale[d:d + 1, :] = wet_dt * geo_ref[d:d + 1, :]
    for f in range(4):
        dscale[2 + f:3 + f, :] = wet_dt * face_ref[f:f + 1, :]

    src_row = lax.broadcasted_iota(jnp.int32, (2 * elems, elems), 0)
    src_col = lax.broadcasted_iota(jnp.int32, (2 * elems, elems), 1)
    itself = jnp.where(src_row == src_col, 1.0, 0.0)
    for f in range(4):
        nb = nb_ref[f:f + 1, :]
        local = nb - me * elems
        row = jnp.where(local < 0, local + elems + RIVW, jnp.where(local < elems, local, local + elems - RIVW))
        row = jnp.where(nb >= 0, row, -1)
        hit = jnp.where(src_row == row, 1.0, 0.0)
        own = jnp.where(nb >= 0, 1.0, 0.0) * itself
        sel[:, f * elems:(f + 1) * elems] = (hit - own).astype(BF16)

    for b in range(6):
        block = vol_ref[b] if b < 2 else fb_ref[b - 2]
        hi, lo = split_two(block)
        w_all[0:nodes, b * nodes:(b + 1) * nodes] = hi
        w_all[nodes:2 * nodes, b * nodes:(b + 1) * nodes] = lo

    first = None
    for m in range(members):
        for c in range(1, comps):
            term = work(m, c, lam[m, c])
            first = term if first is None else first + term
    acc[...] = first

    slot_lanes = 128
    chunk = min(npatch, 128)
    tri = jnp.where(
        lax.broadcasted_iota(jnp.int32, (chunk, chunk), 0)
        < lax.broadcasted_iota(jnp.int32, (chunk, chunk), 1), 1.0, 0.0,
    )
    slot = lax.broadcasted_iota(jnp.int32, (slot_lanes, chunk), 0).astype(F32)
    before = jnp.zeros((1, 1), F32)
    for k in range(npatch // chunk):
        mine = jnp.where(po_ref[:, k * chunk:(k + 1) * chunk] == me, 1.0, 0.0)
        rank = jnp.dot(jnp.broadcast_to(mine, (8, chunk)), tri, preferred_element_type=F32)[0:1] + before
        table[k] = jnp.where(slot == rank, 1.0, 0.0) * mine
        before = before + jnp.sum(mine, axis=1, keepdims=True)

    mix = [[[mix_ref[a, d, c] for c in range(comps)] for a in range(comps)] for d in range(2)]

    last = 2 * STEPS - 1

    def stage_group(stage, group):
        for m in group:
            receive(stage, m)
        half = stage % 2
        src = lam if half == 0 else hal
        states = [[src[m, c] for c in range(comps)] for m in group]
        ghost = []
        for m in group:
            for c in range(comps):
                west = rcv[stage, 0, m, c * prows:(c + 1) * prows, :]
                east = rcv[stage, 1, m, c * prows:(c + 1) * prows, :]
                for g in range(groups):
                    a, b = (-RIVW * g) % elems, (elems - RIVW - RIVW * g) % elems
                    wr = pltpu.roll(west, a, 1) if a else west
                    er = pltpu.roll(east, b, 1) if b else east
                    ghost.append(jnp.where(lane < elems // 2, wr, er))
        flat = [x for state in states for x in state]
        full = jnp.concatenate(
            [jnp.concatenate(flat, axis=0), jnp.concatenate(ghost, axis=0)], axis=1
        )
        hi, lo = split_two(full)
        jump = jnp.dot(hi, sel[...], preferred_element_type=F32)
        jump = jump + jnp.dot(lo, sel[...], preferred_element_type=F32)
        cols_hi, cols_lo = [], []
        for i, state in enumerate(states):
            for c in range(comps):
                pieces = []
                for d in range(2):
                    z = mix[d][0][c] * state[0] + mix[d][1][c] * state[1] + mix[d][2][c] * state[2]
                    pieces.append(dscale[d:d + 1, :] * z)
                r = (i * comps + c) * nodes
                for f in range(4):
                    pieces.append(
                        dscale[2 + f:3 + f, :] * jump[r:r + nodes, f * elems:(f + 1) * elems]
                    )
                data = jnp.concatenate(pieces, axis=0)
                dh, dl = split_two(data)
                cols_hi.append(dh)
                cols_lo.append(dl)
        data_hi = jnp.concatenate(cols_hi, axis=1)
        data_lo = jnp.concatenate(cols_lo, axis=1)
        both = jnp.dot(w_all[...], data_hi, preferred_element_type=F32)
        total = both[:nodes] + both[nodes:]
        total = total + jnp.dot(w_all[0:nodes, :], data_lo, preferred_element_type=F32)
        results = []
        for i, (m, state) in enumerate(zip(group, states)):
            new = []
            for c in range(comps):
                k = i * comps + c
                inc = total[:, k * elems:(k + 1) * elems]
                if c > 0:
                    inc = inc - damp[...] * state[c]
                moved = state[c] + inc
                if half:
                    moved = 0.5 * lam[m, c] + 0.5 * moved
                new.append(moved)
            results.append(new)
        dst = lam if half else hal
        for m, new in zip(group, results):
            for c in range(comps):
                if stage < last:
                    pack(stage + 1, m, c, new[c])
                dst[m, c] = new[c]
            if stage < last:
                send(stage + 1, m)
            else:
                out_copy(m).start()
        if stage < last:
            terms = acc[...]
            for m, new in zip(group, results):
                terms = terms + (work(m, 1, new[1]) + work(m, 2, new[2]))
            acc[...] = terms

    def out_copy(m):
        return pltpu.make_async_copy(lam.at[m], out_ref.at[m], out_sem.at[m])

    def run(stage, lo, hi):
        size = min(GROUP, hi - lo)

        def step(i, carry):
            stage_group(stage, [lo + i * size + k for k in range(size)])
            return carry

        count = (hi - lo) // size
        if count == 1:
            step(0, 0)
        else:
            lax.fori_loop(0, count, step, 0)

    def patch_copy(phase, k):
        mine = phases[phase][2]
        return pltpu.make_async_remote_copy(
            src_ref=psnd.at[phase],
            dst_ref=prcv.at[phase, mine],
            send_sem=psnd_sem.at[phase, k],
            recv_sem=prcv_sem.at[phase, k],
            device_id=partner(phase, k),
            device_id_type=NAMED,
        )

    def patch_send(phase, value):
        psnd[phase] = value
        prcv[phase, phases[phase][2]] = value
        for k in range(1, phases[phase][1]):
            patch_copy(phase, k).start()

    def patch_sum(phase):
        for k in range(1, phases[phase][1]):
            patch_copy(phase, k).wait_recv()
        total = prcv[phase, 0]
        for k in range(1, phases[phase][1]):
            total = total + prcv[phase, k]
        return total

    for stage in range(last):
        run(stage, 0, members)

    per_element = jnp.sum(fric_ref[...] * acc[...], axis=0, keepdims=True) * (-2.0 * wet * rough)
    sums = lax.dot_general(
        jnp.broadcast_to(per_element, (8, elems)), onehot[...], (((1,), (1,)), ((), ())),
        precision=FINEST, preferred_element_type=F32,
    )
    patch_send(0, sums)
    half_way = min(1, members)
    run(last, 0, half_way)
    for phase in range(1, len(phases)):
        patch_send(phase, patch_sum(phase - 1))
    run(last, half_way, members)
    sums = patch_sum(len(phases) - 1) * (1.0 / (members_all * nodes))

    result = jnp.zeros((8, slot_lanes), F32)
    for k in range(npatch // chunk):
        result = result + lax.dot_general(
            sums[:, k * chunk:(k + 1) * chunk], table[k], (((1,), (1,)), ((), ())),
            precision=FINEST, preferred_element_type=F32,
        )
    own_ref[...] = result[0:1, :OWN_MAX]

    for m in range(members):
        out_copy(m).wait()
    for stage in range(2 * STEPS):
        for m in range(members):
            @pl.when(me < n_reach - 1)
            def _(stage=stage, m=m):
                halo_copy(stage, 0, m).wait_send()

            @pl.when(me > 0)
            def _(stage=stage, m=m):
                halo_copy(stage, 1, m).wait_send()
    for phase in range(len(phases)):
        for k in range(1, phases[phase][1]):
            patch_copy(phase, k).wait_send()


def shards(
    n_reach, n_ens,
    adjoint, momentum, friction, roughness, geometry, face_scale, vol_blocks, face_blocks,
    flux_mix, neighbours, patch_map, patch_owner, wet,
):
    members, comps, nodes, elems = adjoint.shape
    npatch = roughness.shape[0]
    stages = 2 * STEPS
    prow = comps * nodes * RIVW // elems
    sizes = [n_ens] + radices(n_reach)
    vmem = pl.BlockSpec(memory_space=pltpu.VMEM)
    specs = [pl.BlockSpec(memory_space=pltpu.HBM)] * 13
    finals, owned = pl.pallas_call(
        functools.partial(kernel, n_reach, n_ens, members * n_ens),
        out_shape=(
            jax.ShapeDtypeStruct(adjoint.shape, F32),
            jax.ShapeDtypeStruct((1, OWN_MAX), F32),
        ),
        in_specs=specs,
        out_specs=(pl.BlockSpec(memory_space=pltpu.HBM), vmem),
        scratch_shapes=[
            pltpu.VMEM(momentum.shape, momentum.dtype),
            pltpu.VMEM(friction.shape, F32),
            pltpu.VMEM((1, npatch), F32),
            pltpu.VMEM(geometry.shape, F32),
            pltpu.VMEM(face_scale.shape, F32),
            pltpu.VMEM(vol_blocks.shape, F32),
            pltpu.VMEM(face_blocks.shape, F32),
            pltpu.SMEM((comps, 2, comps), F32),
            pltpu.VMEM(neighbours.shape, jnp.int32),
            pltpu.VMEM((1, elems), jnp.int32),
            pltpu.VMEM((1, npatch), jnp.int32),
            pltpu.VMEM((1, elems), jnp.int32),
            pltpu.SemaphoreType.DMA((members + 12,)),
            pltpu.VMEM(adjoint.shape, F32),
            pltpu.VMEM(adjoint.shape, F32),
            pltpu.VMEM((nodes, elems), F32),
            pltpu.VMEM((2 * elems, 4 * elems), BF16),
            pltpu.VMEM((2 * nodes, 6 * nodes), BF16),
            pltpu.VMEM((8, elems), F32),
            pltpu.VMEM((nodes, elems), F32),
            pltpu.VMEM((npatch, elems), F32),
            pltpu.VMEM((stages, 2, members, prow, elems), F32),
            pltpu.VMEM((stages, 2, members, prow, elems), F32),
            pltpu.VMEM((len(sizes), 8, npatch), F32),
            pltpu.VMEM((len(sizes), max(sizes), 8, npatch), F32),
            pltpu.SemaphoreType.DMA((stages, 2, members)),
            pltpu.SemaphoreType.DMA((stages, 2, members)),
            pltpu.SemaphoreType.DMA((len(sizes), max(sizes))),
            pltpu.SemaphoreType.DMA((len(sizes), max(sizes))),
            pltpu.VMEM((max(npatch // 128, 1), 128, min(npatch, 128)), F32),
            pltpu.SemaphoreType.DMA((members,)),
        ],
        compiler_params=pltpu.CompilerParams(
            collective_id=0, has_side_effects=True, vmem_limit_bytes=60 * 1024 * 1024
        ),
    )(
        adjoint, momentum, friction, roughness.reshape(1, npatch), geometry, face_scale,
        vol_blocks, face_blocks, flux_mix.transpose(1, 0, 2), neighbours, patch_map.reshape(1, elems),
        patch_owner.reshape(1, npatch), wet.reshape(1, elems),
    )
    return finals, owned.reshape(OWN_MAX)


def solution(mesh):
    return jax.shard_map(
        functools.partial(shards, mesh.shape["reach"], mesh.shape["ens"]),
        mesh=mesh,
        in_specs=(
            P("ens", None, None, "reach"),
            P("ens", None, None, "reach"),
            P(None, "reach"),
            P(),
            P(None, "reach"),
            P(None, "reach"),
            P(),
            P(),
            P(),
            P(None, "reach"),
            P("reach"),
            P(),
            P("reach"),
        ),
        out_specs=(P("ens", None, None, "reach"), P("reach")),
        check_vma=False,
    )
```

```python
import functools

import jax
import jax.numpy as jnp
from jax import lax
from jax.experimental import pallas as pl
from jax.experimental.pallas import tpu as pltpu
from jax.sharding import PartitionSpec as P

RIVW = 32
STEPS = 2
OWN_MAX = 32
TIME_STEP = 0.05
F32 = jnp.float32
BF16 = jnp.bfloat16
GROUP = 1
FINEST = lax.Precision.HIGHEST
NAMED = pl.DeviceIdType.MESH


def split_two(x):
    hi = x.astype(BF16)
    return hi, (x - hi.astype(F32)).astype(BF16)


def radices(count):
    out = []
    while count > 1:
        size = next(r for r in (8, 7, 6, 5, 4, 3, 2, count) if count % r == 0)
        out.append(size)
        count //= size
    return out


def kernel(
    n_reach, n_ens, members_all,
    adj_hbm, mom_hbm, fric_hbm, rough_hbm, geo_hbm, face_hbm, vol_hbm, fb_hbm, mix_hbm,
    nb_hbm, pm_hbm, po_hbm, wet_hbm,
    out_ref, own_ref,
    mom_ref, fric_ref, rough_ref, geo_ref, face_ref, vol_ref, fb_ref, mix_ref,
    nb_ref, pm_ref, po_ref, wet_ref, in_sem,
    lam, hal, acc, sel, w_all, dscale, damp, onehot, snd, rcv, psnd, prcv,
    snd_sem, rcv_sem, psnd_sem, prcv_sem, table, out_sem,
):
    members, comps, nodes, elems = lam.shape
    npatch = rough_ref.shape[1]
    me = lax.axis_index("reach")
    my_ens = lax.axis_index("ens")
    groups = elems // RIVW
    prows = nodes // groups
    digits = radices(n_reach)

    phases = [("ens", n_ens, my_ens, 1)]
    if n_reach * n_ens <= 32:
        phases = [("both", n_reach * n_ens, me * n_ens + my_ens, 1)]
        digits = []
    stride = 1
    for size in digits:
        phases.append(("reach", size, lax.rem(lax.div(me, stride), size), stride))
        stride *= size

    def partner(phase, k):
        axis, size, mine, step = phases[phase]
        if axis == "both":
            other = lax.rem(mine + k, size)
            return {"reach": lax.div(other, n_ens), "ens": lax.rem(other, n_ens)}
        other = lax.rem(mine + k, size)
        base = my_ens if axis == "ens" else me
        return {axis: base + (other - mine) * step}

    barrier = pltpu.get_barrier_semaphore()
    expected = 0
    for phase in range(len(phases)):
        for k in range(1, phases[phase][1]):
            pl.semaphore_signal(barrier, inc=1, device_id=partner(phase, k), device_id_type=NAMED)
            expected += 1
    far = len(digits) > 1
    if far:
        @pl.when(me > 0)
        def _():
            pl.semaphore_signal(barrier, inc=1, device_id={"reach": me - 1}, device_id_type=NAMED)

        @pl.when(me < n_reach - 1)
        def _():
            pl.semaphore_signal(barrier, inc=1, device_id={"reach": me + 1}, device_id_type=NAMED)

    state_in = [
        pltpu.make_async_copy(adj_hbm.at[m], lam.at[m], in_sem.at[m]) for m in range(members)
    ]
    tables_in = [
        pltpu.make_async_copy(src, dst, in_sem.at[members + i])
        for i, (src, dst) in enumerate([
            (nb_hbm, nb_ref), (pm_hbm, pm_ref), (rough_hbm, rough_ref), (wet_hbm, wet_ref),
            (fric_hbm, fric_ref), (geo_hbm, geo_ref), (face_hbm, face_ref),
            (vol_hbm, vol_ref), (fb_hbm, fb_ref), (mom_hbm, mom_ref), (mix_hbm, mix_ref),
            (po_hbm, po_ref),
        ])
    ]
    for copy in state_in + tables_in:
        copy.start()

    lane = lax.broadcasted_iota(jnp.int32, (prows, elems), 1)

    def halo_copy(stage, side, m):
        to = me + 1 if side == 0 else me - 1
        return pltpu.make_async_remote_copy(
            src_ref=snd.at[stage, side, m],
            dst_ref=rcv.at[stage, side, m],
            send_sem=snd_sem.at[stage, side, m],
            recv_sem=rcv_sem.at[stage, side, m],
            device_id={"reach": to},
            device_id_type=NAMED,
        )

    def pack(stage, m, c, x):
        for side in range(2):
            packed = None
            for g in range(groups):
                rows = x[g * prows:(g + 1) * prows]
                shift = (RIVW * g - (elems - RIVW if side == 0 else 0)) % elems
                moved = pltpu.roll(rows, shift, 1) if shift else rows
                packed = moved if packed is None else jnp.where(lane >= g * RIVW, moved, packed)
            snd[stage, side, m, c * prows:(c + 1) * prows, :] = packed

    def send(stage, m):
        @pl.when(me < n_reach - 1)
        def _():
            halo_copy(stage, 0, m).start()

        @pl.when(me > 0)
        def _():
            halo_copy(stage, 1, m).start()

    def receive(stage, m):
        @pl.when(me > 0)
        def _():
            halo_copy(stage, 0, m).wait_recv()

        @pl.when(me < n_reach - 1)
        def _():
            halo_copy(stage, 1, m).wait_recv()

    def work(m, c, x):
        if c == 0:
            return None
        return mom_ref[m, c - 1].astype(F32) * x

    for m in range(members):
        state_in[m].wait()
        for c in range(comps):
            pack(0, m, c, lam[m, c])
        if m == 0:
            pl.semaphore_wait(barrier, expected)
            if far:
                @pl.when(me > 0)
                def _():
                    pl.semaphore_wait(barrier, 1)

                @pl.when(me < n_reach - 1)
                def _():
                    pl.semaphore_wait(barrier, 1)
        send(0, m)

    @pl.when(me == 0)
    def _():
        rcv[:, 0] = jnp.zeros(rcv.shape[:1] + rcv.shape[2:], F32)

    @pl.when(me == n_reach - 1)
    def _():
        rcv[:, 1] = jnp.zeros(rcv.shape[:1] + rcv.shape[2:], F32)

    for copy in tables_in:
        copy.wait()
    wet = wet_ref[...].astype(F32)
    wet_dt = TIME_STEP * wet
    patch_row = lax.broadcasted_iota(jnp.int32, (npatch, elems), 0)
    onehot[...] = jnp.where(patch_row == pm_ref[...], 1.0, 0.0).astype(F32)
    rough8 = jnp.broadcast_to(rough_ref[...], (8, npatch))
    rough = jnp.dot(rough8, onehot[...], precision=FINEST, preferred_element_type=F32)[0:1]
    damp[...] = (wet_dt * rough * rough) * fric_ref[...]
    for d in range(2):
        dscale[d:d + 1, :] = wet_dt * geo_ref[d:d + 1, :]
    for f in range(4):
        dscale[2 + f:3 + f, :] = wet_dt * face_ref[f:f + 1, :]

    src_row = lax.broadcasted_iota(jnp.int32, (2 * elems, elems), 0)
    src_col = lax.broadcasted_iota(jnp.int32, (2 * elems, elems), 1)
    itself = jnp.where(src_row == src_col, 1.0, 0.0)
    for f in range(4):
        nb = nb_ref[f:f + 1, :]
        local = nb - me * elems
        row = jnp.where(local < 0, local + elems + RIVW, jnp.where(local < elems, local, local + elems - RIVW))
        row = jnp.where(nb >= 0, row, -1)
        hit = jnp.where(src_row == row, 1.0, 0.0)
        own = jnp.where(nb >= 0, 1.0, 0.0) * itself
        sel[:, f * elems:(f + 1) * elems] = (hit - own).astype(BF16)

    for b in range(6):
        block = vol_ref[b] if b < 2 else fb_ref[b - 2]
        hi, lo = split_two(block)
        w_all[0:nodes, b * nodes:(b + 1) * nodes] = hi
        w_all[nodes:2 * nodes, b * nodes:(b + 1) * nodes] = lo

    first = None
    for m in range(members):
        for c in range(1, comps):
            term = work(m, c, lam[m, c])
            first = term if first is None else first + term
    acc[...] = first

    slot_lanes = 128
    chunk = min(npatch, 128)
    tri = jnp.where(
        lax.broadcasted_iota(jnp.int32, (chunk, chunk), 0)
        < lax.broadcasted_iota(jnp.int32, (chunk, chunk), 1), 1.0, 0.0,
    )
    slot = lax.broadcasted_iota(jnp.int32, (slot_lanes, chunk), 0).astype(F32)
    before = jnp.zeros((1, 1), F32)
    for k in range(npatch // chunk):
        mine = jnp.where(po_ref[:, k * chunk:(k + 1) * chunk] == me, 1.0, 0.0)
        rank = jnp.dot(jnp.broadcast_to(mine, (8, chunk)), tri, preferred_element_type=F32)[0:1] + before
        table[k] = jnp.where(slot == rank, 1.0, 0.0) * mine
        before = before + jnp.sum(mine, axis=1, keepdims=True)

    mix = [[[mix_ref[a, d, c] for c in range(comps)] for a in range(comps)] for d in range(2)]

    last = 2 * STEPS - 1

    def stage_group(stage, group):
        for m in group:
            receive(stage, m)
        half = stage % 2
        src = lam if half == 0 else hal
        states = [[src[m, c] for c in range(comps)] for m in group]
        ghost = []
        for m in group:
            for c in range(comps):
                west = rcv[stage, 0, m, c * prows:(c + 1) * prows, :]
                east = rcv[stage, 1, m, c * prows:(c + 1) * prows, :]
                for g in range(groups):
                    a, b = (-RIVW * g) % elems, (elems - RIVW - RIVW * g) % elems
                    wr = pltpu.roll(west, a, 1) if a else west
                    er = pltpu.roll(east, b, 1) if b else east
                    ghost.append(jnp.where(lane < elems // 2, wr, er))
        flat = [x for state in states for x in state]
        full = jnp.concatenate(
            [jnp.concatenate(flat, axis=0), jnp.concatenate(ghost, axis=0)], axis=1
        )
        hi, lo = split_two(full)
        jump = jnp.dot(hi, sel[...], preferred_element_type=F32)
        jump = jump + jnp.dot(lo, sel[...], preferred_element_type=F32)
        cols_hi, cols_lo = [], []
        for i, state in enumerate(states):
            for c in range(comps):
                pieces = []
                for d in range(2):
                    z = mix[d][0][c] * state[0] + mix[d][1][c] * state[1] + mix[d][2][c] * state[2]
                    pieces.append(dscale[d:d + 1, :] * z)
                r = (i * comps + c) * nodes
                for f in range(4):
                    pieces.append(
                        dscale[2 + f:3 + f, :] * jump[r:r + nodes, f * elems:(f + 1) * elems]
                    )
                data = jnp.concatenate(pieces, axis=0)
                dh, dl = split_two(data)
                cols_hi.append(dh)
                cols_lo.append(dl)
        data_hi = jnp.concatenate(cols_hi, axis=1)
        data_lo = jnp.concatenate(cols_lo, axis=1)
        both = jnp.dot(w_all[...], data_hi, preferred_element_type=F32)
        total = both[:nodes] + both[nodes:]
        total = total + jnp.dot(w_all[0:nodes, :], data_lo, preferred_element_type=F32)
        results = []
        for i, (m, state) in enumerate(zip(group, states)):
            new = []
            for c in range(comps):
                k = i * comps + c
                inc = total[:, k * elems:(k + 1) * elems]
                if c > 0:
                    inc = inc - damp[...] * state[c]
                moved = state[c] + inc
                if half:
                    moved = 0.5 * lam[m, c] + 0.5 * moved
                new.append(moved)
            results.append(new)
        dst = lam if half else hal
        for m, new in zip(group, results):
            for c in range(comps):
                if stage < last:
                    pack(stage + 1, m, c, new[c])
                dst[m, c] = new[c]
            if stage < last:
                send(stage + 1, m)
            else:
                out_copy(m).start()
        if stage < last:
            terms = acc[...]
            for m, new in zip(group, results):
                terms = terms + (work(m, 1, new[1]) + work(m, 2, new[2]))
            acc[...] = terms

    def out_copy(m):
        return pltpu.make_async_copy(lam.at[m], out_ref.at[m], out_sem.at[m])

    def run(stage, lo, hi):
        size = min(GROUP, hi - lo)

        def step(i, carry):
            stage_group(stage, [lo + i * size + k for k in range(size)])
            return carry

        count = (hi - lo) // size
        if count == 1:
            step(0, 0)
        else:
            lax.fori_loop(0, count, step, 0)

    def patch_copy(phase, k):
        mine = phases[phase][2]
        return pltpu.make_async_remote_copy(
            src_ref=psnd.at[phase],
            dst_ref=prcv.at[phase, mine],
            send_sem=psnd_sem.at[phase, k],
            recv_sem=prcv_sem.at[phase, k],
            device_id=partner(phase, k),
            device_id_type=NAMED,
        )

    def patch_send(phase, value):
        psnd[phase] = value
        prcv[phase, phases[phase][2]] = value
        for k in range(1, phases[phase][1]):
            patch_copy(phase, k).start()

    def patch_sum(phase):
        for k in range(1, phases[phase][1]):
            patch_copy(phase, k).wait_recv()
        total = prcv[phase, 0]
        for k in range(1, phases[phase][1]):
            total = total + prcv[phase, k]
        return total

    for stage in range(last):
        run(stage, 0, members)

    per_element = jnp.sum(fric_ref[...] * acc[...], axis=0, keepdims=True) * (-2.0 * wet * rough)
    sums = lax.dot_general(
        jnp.broadcast_to(per_element, (8, elems)), onehot[...], (((1,), (1,)), ((), ())),
        precision=FINEST, preferred_element_type=F32,
    )
    patch_send(0, sums)
    half_way = min(1, members)
    run(last, 0, half_way)
    for phase in range(1, len(phases)):
        patch_send(phase, patch_sum(phase - 1))
    run(last, half_way, members)
    sums = patch_sum(len(phases) - 1) * (1.0 / (members_all * nodes))

    result = jnp.zeros((8, slot_lanes), F32)
    for k in range(npatch // chunk):
        result = result + lax.dot_general(
            sums[:, k * chunk:(k + 1) * chunk], table[k], (((1,), (1,)), ((), ())),
            precision=FINEST, preferred_element_type=F32,
        )
    own_ref[...] = result[0:1, :OWN_MAX]

    for m in range(members):
        out_copy(m).wait()
    for stage in range(2 * STEPS):
        for m in range(members):
            @pl.when(me < n_reach - 1)
            def _(stage=stage, m=m):
                halo_copy(stage, 0, m).wait_send()

            @pl.when(me > 0)
            def _(stage=stage, m=m):
                halo_copy(stage, 1, m).wait_send()
    for phase in range(len(phases)):
        for k in range(1, phases[phase][1]):
            patch_copy(phase, k).wait_send()


def shards(
    n_reach, n_ens,
    adjoint, momentum, friction, roughness, geometry, face_scale, vol_blocks, face_blocks,
    flux_mix, neighbours, patch_map, patch_owner, wet,
):
    members, comps, nodes, elems = adjoint.shape
    npatch = roughness.shape[0]
    stages = 2 * STEPS
    prow = comps * nodes * RIVW // elems
    sizes = [n_ens] + radices(n_reach)
    if n_reach * n_ens <= 32:
        sizes = [n_reach * n_ens]
    vmem = pl.BlockSpec(memory_space=pltpu.VMEM)
    specs = [pl.BlockSpec(memory_space=pltpu.HBM)] * 13
    finals, owned = pl.pallas_call(
        functools.partial(kernel, n_reach, n_ens, members * n_ens),
        out_shape=(
            jax.ShapeDtypeStruct(adjoint.shape, F32),
            jax.ShapeDtypeStruct((1, OWN_MAX), F32),
        ),
        in_specs=specs,
        out_specs=(pl.BlockSpec(memory_space=pltpu.HBM), vmem),
        scratch_shapes=[
            pltpu.VMEM(momentum.shape, momentum.dtype),
            pltpu.VMEM(friction.shape, F32),
            pltpu.VMEM((1, npatch), F32),
            pltpu.VMEM(geometry.shape, F32),
            pltpu.VMEM(face_scale.shape, F32),
            pltpu.VMEM(vol_blocks.shape, F32),
            pltpu.VMEM(face_blocks.shape, F32),
            pltpu.SMEM((comps, 2, comps), F32),
            pltpu.VMEM(neighbours.shape, jnp.int32),
            pltpu.VMEM((1, elems), jnp.int32),
            pltpu.VMEM((1, npatch), jnp.int32),
            pltpu.VMEM((1, elems), jnp.int32),
            pltpu.SemaphoreType.DMA((members + 12,)),
            pltpu.VMEM(adjoint.shape, F32),
            pltpu.VMEM(adjoint.shape, F32),
            pltpu.VMEM((nodes, elems), F32),
            pltpu.VMEM((2 * elems, 4 * elems), BF16),
            pltpu.VMEM((2 * nodes, 6 * nodes), BF16),
            pltpu.VMEM((8, elems), F32),
            pltpu.VMEM((nodes, elems), F32),
            pltpu.VMEM((npatch, elems), F32),
            pltpu.VMEM((stages, 2, members, prow, elems), F32),
            pltpu.VMEM((stages, 2, members, prow, elems), F32),
            pltpu.VMEM((len(sizes), 8, npatch), F32),
            pltpu.VMEM((len(sizes), max(sizes), 8, npatch), F32),
            pltpu.SemaphoreType.DMA((stages, 2, members)),
            pltpu.SemaphoreType.DMA((stages, 2, members)),
            pltpu.SemaphoreType.DMA((len(sizes), max(sizes))),
            pltpu.SemaphoreType.DMA((len(sizes), max(sizes))),
            pltpu.VMEM((max(npatch // 128, 1), 128, min(npatch, 128)), F32),
            pltpu.SemaphoreType.DMA((members,)),
        ],
        compiler_params=pltpu.CompilerParams(
            collective_id=0, has_side_effects=True, vmem_limit_bytes=60 * 1024 * 1024
        ),
    )(
        adjoint, momentum, friction, roughness.reshape(1, npatch), geometry, face_scale,
        vol_blocks, face_blocks, flux_mix.transpose(1, 0, 2), neighbours, patch_map.reshape(1, elems),
        patch_owner.reshape(1, npatch), wet.reshape(1, elems),
    )
    return finals, owned.reshape(OWN_MAX)


def solution(mesh):
    return jax.shard_map(
        functools.partial(shards, mesh.shape["reach"], mesh.shape["ens"]),
        mesh=mesh,
        in_specs=(
            P("ens", None, None, "reach"),
            P("ens", None, None, "reach"),
            P(None, "reach"),
            P(),
            P(None, "reach"),
            P(None, "reach"),
            P(),
            P(),
            P(),
            P(None, "reach"),
            P("reach"),
            P(),
            P("reach"),
        ),
        out_specs=(P("ens", None, None, "reach"), P("reach")),
        check_vma=False,
    )
```
